256 devices in a mesh: prow: 16 (over z, core), pcol: 16 (over y, x).
Axes of the slice: x: 4, y: 4, z: 8, core: 2. Of those that a mesh axis runs over, the one named last changes fastest.
Arguments:
- matrix: float32 [1, 8192, 1, 8192], P(None, 'prow', None, 'pcol'), may hold values from -6 to 6
- pivots: int32 [2, 512], replicated, may hold values from 1024 to 8191, as said below
- lower_inv: float32 [2, 512, 512], replicated, as said below
- upper_inv: float32 [2, 512, 512], replicated, as said below
Outputs:
- factored: float32 [1, 8192, 1, 8192], P(None, 'prow', None, 'pcol')
The draws below stay inside these ranges and needn't reach their ends.
Inputs may be any that keep to these rules, and one draw needn't show every extreme that they name: `pivots`: in step k the 512 entries are distinct rows; at most 37 of them lie in rows held by one index of prow, and exactly 37 for some index. `lower_inv`: each of the 2 matrices is unit lower triangular. `upper_inv`: each of the 2 matrices is upper triangular with a nonzero diagonal.
All inputs are finite; a program needn't handle non-finite values.
Results may differ from the reference program's by a relative error of at most 0.0001.
Values sent between devices are 32-bit elements; how exact they have to be, the bound alone decides.
A program may use at most 64 MiB of HBM per device.

```python
import math
import jax
import jax.numpy as jnp
from jax import lax

NB = 512
BLK = 1
STEPS = 2
ROWS = 8192
COLS = 8192
CAP = 37
N_PROW = 16
N_PCOL = 16


def draw_pivots(key, part):
    groups = N_PROW - STEPS
    local_count = BLK * NB
    result = []
    for step in range(STEPS):
        step_key = jax.random.fold_in(key, 11 + step)
        full_group = jax.random.randint(jax.random.fold_in(step_key, 1), (), 0, groups)
        slot_perm = jax.random.permutation(jax.random.fold_in(step_key, 2), groups * CAP)
        slot_pos = jnp.argsort(slot_perm).astype(jnp.int32)
        slot_ids = jnp.arange(groups * CAP).astype(jnp.int32)
        slot_group = slot_ids // CAP
        scores = jnp.where(slot_group == full_group, slot_ids - 2 * groups * CAP, slot_pos)
        order = jnp.argsort(scores, stable=True).astype(jnp.int32)
        taken = order[:NB]
        tables = []
        for group in range(groups):
            tables.append(jax.random.permutation(jax.random.fold_in(step_key, 100 + group), local_count)[:CAP])
        table = jnp.stack(tables).astype(jnp.int32)
        taken_group = taken // CAP
        taken_slot = taken % CAP
        local_row = table[taken_group, taken_slot]
        owner = taken_group + STEPS
        rows = (local_row // NB * N_PROW + owner) * NB + local_row % NB
        mixing = jax.random.permutation(jax.random.fold_in(step_key, 3), NB)
        result.append(rows[mixing].astype(jnp.int32))
    return jnp.stack(result).astype(jnp.int32)


def draw_lower_inv(key, part):
    shape = (STEPS, NB, NB)
    row_index = jnp.arange(NB)[:, None]
    col_index = jnp.arange(NB)[None, :]
    spread_part = 0.5 * jax.random.normal(key, shape, jnp.float32) / math.sqrt(NB)
    diagonal = jnp.where(row_index == col_index, 1.0, 0.0).astype(jnp.float32)
    return jnp.where(row_index > col_index, spread_part, diagonal).astype(jnp.float32)


def draw_upper_inv(key, part):
    shape = (STEPS, NB, NB)
    row_index = jnp.arange(NB)[:, None]
    col_index = jnp.arange(NB)[None, :]
    key_off = jax.random.fold_in(key, 21)
    key_mag = jax.random.fold_in(key, 22)
    key_sign = jax.random.fold_in(key, 23)
    spread_part = 0.03 * jax.random.normal(key_off, shape, jnp.float32) / math.sqrt(NB)
    magnitude = jnp.exp(jax.random.uniform(key_mag, shape, jnp.float32, math.log(0.01), math.log(0.05)))
    signs = jnp.where(jax.random.bernoulli(key_sign, 0.5, shape), 1.0, -1.0).astype(jnp.float32)
    diagonal = magnitude * signs
    upper_vals = jnp.where(row_index < col_index, spread_part, 0.0)
    return jnp.where(row_index == col_index, diagonal, upper_vals).astype(jnp.float32)


def block_levels(key, dims, split, low, high):
    loudness, own = 1.0, jax.random.fold_in(key, 6)
    for dim, shards_of in split:
        draws = jnp.exp(jax.random.uniform(jax.random.fold_in(own, dim), (shards_of,), jnp.float32, low / len(split), high / len(split)))
        loudness = loudness * jnp.repeat(draws, dims[dim] // shards_of).reshape([-1 if axis == dim else 1 for axis in range(len(dims))])
    return loudness


def scatter_about(own_key, extent, width, bound, cuts=(), dtype=jnp.bfloat16):
    factor_of = block_levels(own_key, extent, cuts, -0.22, 0.18) if cuts else 1.0
    values = jax.random.normal(own_key, extent, jnp.float32) * width * factor_of
    return jnp.minimum(jnp.maximum(values, -bound), bound).astype(dtype)


def setup_inputs(seed: int = 0) -> dict:
    keys = jax.random.split(jax.random.key(seed), 5)
    return {
        "matrix": scatter_about(keys[0], (BLK, N_PROW * NB, BLK, N_PCOL * NB), 1.0, 6.0, ((1, 16), (3, 16)), jnp.float32),
        "pivots": draw_pivots(jax.random.fold_in(keys[4], 71), 0),
        "lower_inv": draw_lower_inv(jax.random.fold_in(keys[4], 71), 0),
        "upper_inv": draw_upper_inv(jax.random.fold_in(keys[4], 71), 0),
    }


def reference(matrix, pivots, lower_inv, upper_inv):
    whole = matrix.reshape(ROWS, COLS)
    highest = lax.Precision.HIGHEST
    for step in range(STEPS):
        start = step * NB
        chosen = pivots[step].astype(jnp.int32)
        places = (start + jnp.arange(NB)).astype(jnp.int32)
        row_order = jnp.arange(ROWS).astype(jnp.int32)
        row_order = row_order.at[places].set(chosen)
        row_order = row_order.at[chosen].set(places)
        whole = jnp.take(whole, row_order, axis=0)
        lower_part = jnp.dot(whole[start + NB:, start:start + NB], upper_inv[step], precision=highest)
        upper_part = jnp.dot(lower_inv[step], whole[start:start + NB, start + NB:], precision=highest)
        trailing = whole[start + NB:, start + NB:] - jnp.dot(lower_part, upper_part, precision=highest)
        whole = whole.at[start + NB:, start:start + NB].set(lower_part)
        whole = whole.at[start:start + NB, start + NB:].set(upper_part)
        whole = whole.at[start + NB:, start + NB:].set(trailing)
    return whole.reshape(matrix.shape)
```

```python
import functools

import jax
import jax.numpy as jnp
from jax import lax
from jax.experimental import pallas as pl
from jax.experimental.pallas import tpu as pltpu
from jax.sharding import PartitionSpec as P

MESH = pl.DeviceIdType.MESH
F32 = jnp.float32
BF16 = jnp.bfloat16

N = 512
STEPS = 2
SLOT = 40
HEADS = 2
DEPTH = 640
FIX = 64
PARTS = 3


def dot(a, b):
    return jnp.dot(a, b, preferred_element_type=F32)


def split(v):
    high = v.astype(BF16)
    return high, (v - high.astype(F32)).astype(BF16)


def product(a, b):
    return dot(a[0], b[0]) + (dot(a[0], b[1]) + dot(a[1], b[0]))


def select_rows(chooser, v):
    high = v.astype(BF16)
    rest = v - high.astype(F32)
    mid = rest.astype(BF16)
    low = (rest - mid.astype(F32)).astype(BF16)
    return dot(chooser, high) + (dot(chooser, mid) + dot(chooser, low))


def iota(shape, dim):
    return lax.broadcasted_iota(jnp.int32, shape, dim)


def kernel(
    lin_hbm, piv_ref, linv_hbm, uinv_hbm, out_ref,
    lin, x_ref, li, ui, lsh, lsl, uih, uil, pick, pick_t, slot_row, slot_col,
    pack, f_ref, g_ref, pb, pf, low, upp,
    load_sem, xs, xr, rs, rr, bs, br, ss, sr,
):
    p = lax.axis_index("prow")
    q = lax.axis_index("pcol")
    z, core = p // 2, p % 2
    y, x = q // 4, q % 4
    up_z = lax.rem(z + 1, 8) * 2 + core
    down_z = lax.rem(z + 7, 8) * 2 + core
    sibling = z * 2 + (1 - core)

    def at_x(d):
        return (p, y * 4 + lax.rem(x + d, 4))

    def at_y(d):
        return (p, lax.rem(y + d, 4) * 4 + x)

    barrier = pltpu.get_barrier_semaphore()
    friends = [at_x(1), at_x(2), at_x(3), at_y(1), at_y(2), at_y(3), (up_z, q), (down_z, q), (sibling, q)]
    for friend in friends:
        pl.semaphore_signal(barrier, inc=1, device_id=friend, device_id_type=MESH)

    @pl.when(p >= HEADS)
    def _():
        for head in range(HEADS):
            pl.semaphore_signal(barrier, inc=1, device_id=(head, q), device_id_type=MESH)

    loads = [
        pltpu.make_async_copy(lin_hbm, lin, load_sem.at[0]),
        pltpu.make_async_copy(linv_hbm, li, load_sem.at[1]),
        pltpu.make_async_copy(uinv_hbm, ui, load_sem.at[2]),
    ]
    for load in loads:
        load.start()

    before = (iota((N, N), 0) < iota((N, N), 1)).astype(BF16)
    same = iota((N, N), 0) == iota((N, N), 1)
    first = (p - HEADS) * SLOT
    for s in range(STEPS):
        piv = piv_ref[s : s + 1, :]
        owner = lax.shift_right_logical(piv, 9)
        place = jnp.bitwise_and(piv, N - 1)
        owned = (iota((16, N), 0) == owner).astype(F32)
        rank = jnp.sum(owned * dot(owned.astype(BF16), before), axis=0, keepdims=True)
        slots = ((owner - HEADS) * SLOT).astype(F32) + rank
        slots_down = jnp.sum(jnp.where(same, slots, 0.0), axis=1, keepdims=True)
        place_down = jnp.sum(jnp.where(same, place.astype(F32), 0.0), axis=1, keepdims=True)
        slot_row[s] = slots
        slot_col[s] = slots_down
        mine = (slots == (iota((48, N), 0) + first).astype(F32)).astype(BF16)
        pick[s] = dot(mine, (place_down == iota((N, N), 1).astype(F32)).astype(BF16))[:SLOT]
        across = iota((N, 128), 1)
        mine_t = jnp.logical_and(slots_down == (across + first).astype(F32), across < SLOT)
        pick_t[s] = dot((place.astype(F32) == iota((N, N), 0).astype(F32)).astype(BF16), mine_t.astype(F32).astype(BF16))
        f_ref[s, SLOT:FIX, :] = jnp.zeros((FIX - SLOT, N), F32)
        g_ref[s, 14 * SLOT : DEPTH, :] = jnp.zeros((DEPTH - 14 * SLOT, N), F32)

    loads[0].wait()
    for c in range(4):
        x_ref[:, 128 * c : 128 * (c + 1)] = lin[pl.ds(c, N, stride=4), :]

    @pl.when(p >= HEADS)
    def _():
        pl.semaphore_wait(barrier, len(friends))

    @pl.when(p < HEADS)
    def _():
        pl.semaphore_wait(barrier, len(friends) + 14)

    def remote(src, dst, send, recv, device):
        return pltpu.make_async_remote_copy(
            src_ref=src, dst_ref=dst, send_sem=send, recv_sem=recv, device_id=device, device_id_type=MESH
        )

    def stage(s, carry):
        def rows_of(k, h, i):
            if k < 2:
                return pl.ds(pl.multiple_of(k * 256 + h * 128 + i * 32, 32), 32)
            return pl.ds(pl.multiple_of(h * 32 + i * 8, 8), 8)

        def target(k):
            return pb.at[s] if k < 2 else pf.at[s]

        def source(k):
            return x_ref if k < 2 else f_ref.at[s]

        root = q == s

        def send_index(st, k, h, d):
            return ((st * PARTS + k) * 2 + h) * 3 + d - 1

        def recv_index(st, k, h, d):
            return s * 54 + send_index(st, k, h, d)

        def xy_copy(st, k, h, d):
            if h == 0:
                along_x = st != 1
            else:
                along_x = st == 1
            device = at_x(d) if along_x else at_y(d)
            if st == 0:
                i = lax.rem(x + d, 4) if h == 0 else lax.rem(y + d, 4)
                src = source(k).at[rows_of(k, h, i)]
            else:
                i = x if h == 0 else y
                src = target(k).at[rows_of(k, h, i)]
            dst = target(k).at[rows_of(k, h, i)]
            arrival = d if st == 2 else 1
            return remote(src, dst, xs.at[send_index(st, k, h, d)], xr.at[recv_index(st, k, h, arrival)], device)

        def senders(st, h):
            if st == 0:
                return root
            if st == 1:
                return y == 0 if h == 0 else x == s
            return None

        def receivers(st, h):
            if st == 0:
                return jnp.logical_and(y == 0, x != s) if h == 0 else jnp.logical_and(x == s, y != 0)
            if st == 1:
                return y != 0 if h == 0 else x != s
            return None

        def when(condition, action):
            if condition is None:
                action()
            else:
                pl.when(condition)(action)

        def xy_send(st, k):
            for h in range(2):

                def go(h=h):
                    for d in (1, 2, 3):
                        xy_copy(st, k, h, d).start()

                when(senders(st, h), go)

        def xy_arrive(st, k):
            for h in range(2):

                def go(h=h):
                    for d in (1, 2, 3) if st == 2 else (1,):
                        xy_copy(st, k, h, d).wait_recv()

                when(receivers(st, h), go)

        def xy_sent(st, k):
            for h in range(2):

                def go(h=h):
                    for d in (1, 2, 3):
                        xy_copy(st, k, h, d).wait_send()

                when(senders(st, h), go)

        def xy_keep(k):
            def go():
                for h, i in ((0, x), (1, y)):
                    rows = rows_of(k, h, i)
                    target(k)[rows, :] = source(k)[rows, :]

            pl.when(root)(go)

        def block(zb, lo=0, size=SLOT, c=core):
            return g_ref.at[s, pl.ds(pl.multiple_of((2 * zb + c - HEADS) * SLOT + lo, 8), size)]

        def part(t, side):
            return (0, SLOT) if t < 4 else ((0, 24) if side == 0 else (24, 16))

        def chip(t, side):
            return lax.rem(z + (8 - t if side == 0 else t), 8)

        def ring_copy(t, side, back):
            ref = block(chip(back, side), *part(t, side))
            n = side * 4 + t - 1
            return remote(ref, ref, rs.at[n], rr.at[s * 8 + n], (up_z if side == 0 else down_z, q))

        def core_copy(t, side, c=core):
            ref = block(chip(t, side), *part(t, side), c=c)
            n = 0 if t == 0 else 1 + side * 4 + t - 1
            return remote(ref, ref, bs.at[n], br.at[s * 9 + n], (sibling, q))

        def ring_arrive(t):
            for side in range(2):

                def go(side=side):
                    ring_copy(t, side, t).wait_recv()
                    if t < 4:
                        ring_copy(t + 1, side, t).start()
                    core_copy(t, side).start()

                pl.when(chip(t, side) != 0)(go)

        def scatter_copy(o):
            rows = pl.ds(pl.multiple_of(o * SLOT, 8), SLOT)
            return remote(pack.at[rows], f_ref.at[s, pl.ds(0, SLOT)], ss.at[o], sr.at[s], (o + HEADS, q))

        @pl.when(p == s)
        def _():
            chooser = (slot_row[s] == iota((14 * SLOT, N), 0).astype(F32)).astype(F32).astype(BF16)
            pack[...] = select_rows(chooser, x_ref[...])
            lax.fori_loop(0, 14, lambda o, c: (scatter_copy(o).start(), c)[1], 0)

        @pl.when(z != 0)
        def _():
            g_ref[s, pl.ds(pl.multiple_of((p - HEADS) * SLOT, 8), SLOT), :] = select_rows(
                pick[s].astype(BF16), x_ref[...]
            )
            ring_copy(1, 0, 0).start()
            ring_copy(1, 1, 0).start()
            core_copy(0, 0).start()

        xy_send(0, 0)
        xy_send(0, 1)
        xy_keep(0)
        xy_keep(1)

        @pl.when(s == 0)
        def _():
            loads[1].wait()
            loads[2].wait()

        order = (slot_col[s] == iota((N, DEPTH), 1).astype(F32)).astype(F32).astype(BF16)
        lower = split(li[s])
        lsh[...] = dot(lower[0], order).astype(BF16)
        lsl[...] = dot(lower[1], order).astype(BF16)
        uih[...], uil[...] = split(ui[s])

        ring_arrive(1)
        xy_arrive(0, 0)
        xy_send(1, 0)
        xy_arrive(0, 1)
        xy_send(1, 1)
        ring_arrive(2)

        @pl.when(p >= HEADS)
        def _():
            scatter_copy(0).wait_recv()

        @pl.when(p < HEADS)
        def _():
            f_ref[s, 0:SLOT, :] = jnp.zeros((SLOT, N), F32)

        xy_send(0, 2)
        xy_keep(2)
        xy_arrive(1, 0)
        xy_send(2, 0)
        xy_arrive(0, 2)
        xy_send(1, 2)
        xy_arrive(1, 1)
        xy_send(2, 1)
        ring_arrive(3)
        xy_arrive(1, 2)
        xy_send(2, 2)
        upper_inv = (uih[...], uil[...])
        xy_arrive(2, 0)
        low[0:256, :] = product(split(pb[s, 0:256, :]), upper_inv)
        ring_arrive(4)
        xy_arrive(2, 1)
        low[256:512, :] = product(split(pb[s, 256:512, :]), upper_inv)
        xy_arrive(2, 2)

        chosen_t = pick_t[s].astype(BF16)[:, 0:FIX]
        is_target = jnp.sum(pick_t[s], axis=1, keepdims=True) > 0.5

        @pl.when(p > s)
        def _():
            fixed = product(split(pf[s]), upper_inv)
            low[...] = jnp.where(is_target, select_rows(chosen_t, fixed), low[...])

        for k in range(PARTS):
            for st in range(3):
                xy_sent(st, k)

        @pl.when(p == s)
        def _():
            lax.fori_loop(0, 14, lambda o, c: (scatter_copy(o).wait_send(), c)[1], 0)

        @pl.when(p > s)
        def _():
            x_ref[...] = jnp.where(is_target, select_rows(chosen_t, f_ref[s]), x_ref[...])

        @pl.when(z != 0)
        def _():
            core_copy(0, 0, 1 - core).wait_recv()
            core_copy(0, 0).wait_send()

        for side in range(2):
            for t in (1, 2, 3, 4):

                def arrived(side=side, t=t):
                    core_copy(t, side, 1 - core).wait_recv()
                    core_copy(t, side).wait_send()

                def sent(side=side, t=t):
                    ring_copy(t, side, t - 1).wait_send()

                pl.when(chip(t, side) != 0)(arrived)
                pl.when(chip(t - 1, side) != 0)(sent)

        @pl.when(q > s)
        def _():
            upp[...] = product((lsh[...], lsl[...]), split(g_ref[s]))

        @pl.when(jnp.logical_and(p == s, q <= s))
        def _():
            place = (slot_col[s] == iota((N, DEPTH), 1).astype(F32)).astype(F32).astype(BF16)
            x_ref[...] = select_rows(place, g_ref[s])

        @pl.when(jnp.logical_and(p == s, q > s))
        def _():
            x_ref[...] = upp[...]

        @pl.when(jnp.logical_and(p > s, q == s))
        def _():
            x_ref[...] = low[...]

        @pl.when(jnp.logical_and(p > s, q > s))
        def _():
            x_ref[...] = x_ref[...] - product(split(low[...]), split(upp[...]))

        return carry

    lax.fori_loop(0, STEPS, stage, 0)
    for c in range(4):
        out_ref[pl.ds(c, N, stride=4), :] = x_ref[:, 128 * c : 128 * (c + 1)]


def body(matrix, pivots, lower_inv, upper_inv):
    vm, dma = pltpu.VMEM, pltpu.SemaphoreType.DMA
    any_space = pl.BlockSpec(memory_space=pl.ANY)
    done = pl.pallas_call(
        kernel,
        out_shape=jax.ShapeDtypeStruct((4 * N, 128), F32),
        in_specs=[any_space, pl.BlockSpec(memory_space=vm), any_space, any_space],
        out_specs=pl.BlockSpec(memory_space=vm),
        scratch_shapes=[
            vm((4 * N, 128), F32),
            vm((N, N), F32),
            vm((STEPS, N, N), F32),
            vm((STEPS, N, N), F32),
            vm((N, DEPTH), BF16),
            vm((N, DEPTH), BF16),
            vm((N, N), BF16),
            vm((N, N), BF16),
            vm((STEPS, SLOT, N), F32),
            vm((STEPS, N, 128), F32),
            vm((STEPS, 1, N), F32),
            vm((STEPS, N, 1), F32),
            vm((14 * SLOT, N), F32),
            vm((STEPS, FIX, N), F32),
            vm((STEPS, DEPTH, N), F32),
            vm((STEPS, N, N), F32),
            vm((STEPS, FIX, N), F32),
            vm((N, N), F32),
            vm((N, N), F32),
            dma((3,)),
            dma((54,)),
            dma((108,)),
            dma((8,)),
            dma((16,)),
            dma((9,)),
            dma((18,)),
            dma((14,)),
            dma((STEPS,)),
        ],
        compiler_params=pltpu.CompilerParams(
            collective_id=0, has_side_effects=True, vmem_limit_bytes=56 << 20
        ),
        cost_estimate=pl.CostEstimate(flops=10**10, bytes_accessed=7 << 20, transcendentals=0),
    )(matrix.reshape(4 * N, 128), pivots, lower_inv, upper_inv)
    return done.reshape(matrix.shape)


def solution(mesh):
    placed = (P(None, "prow", None, "pcol"), P(), P(), P())
    return jax.shard_map(
        body, mesh=mesh, in_specs=placed, out_specs=P(None, "prow", None, "pcol"), check_vma=False
    )
```

```python
import functools

import jax
import jax.numpy as jnp
from jax import lax
from jax.experimental import pallas as pl
from jax.experimental.pallas import tpu as pltpu
from jax.sharding import PartitionSpec as P

MESH = pl.DeviceIdType.MESH
F32 = jnp.float32
BF16 = jnp.bfloat16

N = 512
STEPS = 2
SLOT = 40
HEADS = 2
DEPTH = 640
FIX = 48
SIZES = (24, 24, 24, 16, 8)
CHUNKS = len(SIZES) - 1
LONG = 6 * sum(SIZES[:-1])
CUT = 6 * sum(SIZES[:2])
SUB = ((0, 24), (24, 16))
FAR = (6, 7, 4, 5, 8, 9, 2, 3, 10, 11, 0, 1, 12, 13)


def dot(a, b):
    return jnp.dot(a, b, preferred_element_type=F32)


def split(v):
    high = v.astype(BF16)
    return high, (v - high.astype(F32)).astype(BF16)


def product(a, b):
    return dot(a[0], b[0]) + (dot(a[0], b[1]) + dot(a[1], b[0]))


def select_rows(chooser, v):
    high = v.astype(BF16)
    rest = v - high.astype(F32)
    mid = rest.astype(BF16)
    low = (rest - mid.astype(F32)).astype(BF16)
    return dot(chooser, high) + (dot(chooser, mid) + dot(chooser, low))


def iota(shape, dim):
    return lax.broadcasted_iota(jnp.int32, shape, dim)


def kernel(
    lin_hbm, piv_ref, linv_hbm, uinv_hbm, out_ref,
    lin, x_ref, li, ui, lsh, lsl, uih, uil, pick, pick_t, slot_row, slot_col,
    pack, f_ref, g_ref, pb, pf, low, upp,
    load_sem, xs, xr, rs, rr, bs, br, ss, sr,
):
    p = lax.axis_index("prow")
    q = lax.axis_index("pcol")
    z, core = p // 2, p % 2
    y, x = q // 4, q % 4
    along_z = [lax.rem(z + d, 8) * 2 + core for d in (1, 7, 2, 6)]
    sibling = z * 2 + (1 - core)

    def at_x(d):
        return (p, y * 4 + lax.rem(x + d, 4))

    def at_y(d):
        return (p, lax.rem(y + d, 4) * 4 + x)

    barrier = pltpu.get_barrier_semaphore()
    friends = [at_x(1), at_x(2), at_x(3), at_y(1), at_y(2), at_y(3), (sibling, q)]
    friends += [(other, q) for other in along_z]

    @pl.when(p >= HEADS)
    def _():
        for head in range(HEADS):
            pl.semaphore_signal(barrier, inc=1, device_id=(head, q), device_id_type=MESH)

    for friend in friends:
        pl.semaphore_signal(barrier, inc=1, device_id=friend, device_id_type=MESH)

    loads = [
        pltpu.make_async_copy(lin_hbm, lin, load_sem.at[0]),
        pltpu.make_async_copy(linv_hbm, li, load_sem.at[1]),
        pltpu.make_async_copy(uinv_hbm, ui, load_sem.at[2]),
    ]
    for load in loads:
        load.start()

    before = (iota((N, N), 0) < iota((N, N), 1)).astype(BF16)
    same = iota((N, N), 0) == iota((N, N), 1)
    first = (p - HEADS) * SLOT
    empty = jnp.where(z == 0, 0, jnp.where(z < 4, 2 * z - 1, jnp.where(z == 4, 7, 2 * (8 - z))))
    for s in range(STEPS):
        piv = piv_ref[s : s + 1, :]
        owner = lax.shift_right_logical(piv, 9)
        place = jnp.bitwise_and(piv, N - 1)
        owned = (iota((16, N), 0) == owner).astype(F32)
        rank = jnp.sum(owned * dot(owned.astype(BF16), before), axis=0, keepdims=True)
        slots = ((owner - HEADS) * SLOT).astype(F32) + rank
        back = jnp.bitwise_and(z - lax.shift_right_logical(owner, 1), 7)
        turn = jnp.where(back == 0, 0, jnp.where(back < 4, 2 * back - 1, jnp.where(back == 4, 7, 2 * (8 - back))))
        gathered = (turn * (2 * SLOT) + jnp.bitwise_and(owner, 1) * SLOT).astype(F32) + rank
        slots_down = jnp.sum(jnp.where(same, slots, 0.0), axis=1, keepdims=True)
        place_down = jnp.sum(jnp.where(same, place.astype(F32), 0.0), axis=1, keepdims=True)
        slot_row[s] = slots
        slot_col[s] = jnp.sum(jnp.where(same, gathered, 0.0), axis=1, keepdims=True)
        mine = (slots == (iota((48, N), 0) + first).astype(F32)).astype(BF16)
        pick[s] = dot(mine, (place_down == iota((N, N), 1).astype(F32)).astype(BF16))[:SLOT]
        across = iota((N, 128), 1)
        mine_t = jnp.logical_and(slots_down == (across + first).astype(F32), across < SLOT)
        pick_t[s] = dot((place.astype(F32) == iota((N, N), 0).astype(F32)).astype(BF16), mine_t.astype(F32).astype(BF16))
        f_ref[s, SLOT:FIX, :] = jnp.zeros((FIX - SLOT, N), F32)
        g_ref[s, pl.ds(pl.multiple_of(empty * 2 * SLOT, 8), 2 * SLOT), :] = jnp.zeros((2 * SLOT, N), F32)

    x_ref[N:LONG, :] = jnp.zeros((LONG - N, N), F32)
    loads[0].wait()
    for c in range(4):
        x_ref[0:N, 128 * c : 128 * (c + 1)] = lin[pl.ds(c, N, stride=4), :]

    own_rows = pl.ds(pl.multiple_of(core * SLOT, 8), SLOT)

    def choose_own(s):
        @pl.when(z != 0)
        def _():
            g_ref[s, own_rows, :] = select_rows(pick[s].astype(BF16), x_ref[0:N, :])

    def choose_scattered(s):
        @pl.when(p == s)
        def _():
            chooser = (slot_row[s] == iota((14 * SLOT, N), 0).astype(F32)).astype(F32).astype(BF16)
            pack[...] = select_rows(chooser, x_ref[0:N, :])

    choose_own(0)
    choose_scattered(0)

    @pl.when(p >= HEADS)
    def _():
        pl.semaphore_wait(barrier, len(friends))

    @pl.when(p < HEADS)
    def _():
        pl.semaphore_wait(barrier, len(friends) + 14)

    def remote(src, dst, send, recv, device):
        return pltpu.make_async_remote_copy(
            src_ref=src, dst_ref=dst, send_sem=send, recv_sem=recv, device_id=device, device_id_type=MESH
        )

    def stage(s, carry):
        offs = (lax.rem(x - s + 4, 4), y)
        root = q == s

        def rows_of(k, h, d):
            at = 6 * sum(SIZES[:k]) if k < CHUNKS else 0
            return pl.ds(pl.multiple_of(at + (h * 3 + d - 1) * SIZES[k], 8), SIZES[k])

        def target(k):
            return pb.at[s] if k < CHUNKS else pf.at[s]

        def source(k):
            return x_ref if k < CHUNKS else f_ref.at[s]

        def index(st, k, h, d):
            return ((st * (CHUNKS + 1) + k) * 2 + h) * 3 + d - 1

        def xy_copy(st, k, h, d, piece, arrival):
            device = at_x(d) if (h == 0) == (st != 1) else at_y(d)
            rows = rows_of(k, h, piece)
            src = source(k).at[rows] if st == 0 else target(k).at[rows]
            return remote(
                src, target(k).at[rows], xs.at[index(st, k, h, d)],
                xr.at[s * 6 * 3 * (CHUNKS + 1) + index(st, k, h, arrival)], device,
            )

        def each_send(st, k, action):
            for h in range(2):
                mine, other = offs[h], offs[1 - h]
                if st == 0:

                    @pl.when(root)
                    def _(h=h):
                        for d in (1, 2, 3):
                            action(xy_copy(0, k, h, d, d, 1))

                elif st == 1:

                    @pl.when(jnp.logical_and(other == 0, mine != 0))
                    def _(h=h, mine=mine):
                        for d in (1, 2, 3):
                            action(xy_copy(1, k, h, d, mine, 1))

                else:
                    for d in (1, 2, 3):
                        spared = jnp.logical_and(other == 0, lax.rem(mine + d, 4) == 0)

                        @pl.when(jnp.logical_and(mine != 0, jnp.logical_not(spared)))
                        def _(h=h, mine=mine, d=d):
                            action(xy_copy(2, k, h, d, mine, d))

        def xy_send(st, k):
            each_send(st, k, lambda copy: copy.start())

        def xy_sent(st, k):
            each_send(st, k, lambda copy: copy.wait_send())

        def xy_arrive(st, k):
            for h in range(2):
                mine, other = offs[h], offs[1 - h]
                if st == 0:

                    @pl.when(jnp.logical_and(other == 0, mine != 0))
                    def _(h=h, mine=mine):
                        xy_copy(0, k, h, 1, mine, 1).wait_recv()

                elif st == 1:

                    @pl.when(jnp.logical_and(other != 0, mine != 0))
                    def _(h=h, mine=mine):
                        xy_copy(1, k, h, 1, mine, 1).wait_recv()

                else:
                    for d in (1, 2, 3):
                        giver = lax.rem(mine + 4 - d, 4)

                        @pl.when(jnp.logical_and(giver != 0, jnp.logical_not(root)))
                        def _(h=h, d=d, giver=giver):
                            xy_copy(2, k, h, d, giver, d).wait_recv()

        def chip(t, side):
            return lax.rem(z + (8 - t if side == 0 else t), 8)

        def block(t, side, c, part):
            turn = 0 if t == 0 else (7 if t == 4 else 2 * t - 1 + side)
            return g_ref.at[s, pl.ds(pl.multiple_of(turn * 2 * SLOT + c * SLOT + part[0], 8), part[1])]

        def ring_copy(t, side):
            n = side * 4 + t - 1
            part = SUB[side] if t == 4 else (0, SLOT)
            return remote(
                block(0 if t < 3 else 2, side, core, part), block(t, side, core, part),
                rs.at[n], rr.at[s * 8 + n], (along_z[side if t % 2 else 2 + side], q),
            )

        def core_copy(t, side, c=core):
            ref = block(t, side, c, SUB[side] if t == 4 else (0, SLOT))
            n = 0 if t == 0 else 1 + side * 4 + t - 1
            return remote(ref, ref, bs.at[n], br.at[s * 9 + n], (sibling, q))

        def ring_arrive(t):
            for side in range(2):

                @pl.when(chip(t, side) != 0)
                def _(side=side):
                    ring_copy(t, side).wait_recv()
                    if t == 2:
                        ring_copy(3, side).start()
                        ring_copy(4, side).start()
                    core_copy(t, side).start()

        def scatter_copy(o):
            rows = pl.ds(o * SLOT, SLOT)
            return remote(pack.at[rows], f_ref.at[s, pl.ds(0, SLOT)], ss.at[o], sr.at[s], (o + HEADS, q))

        def scatter(owners):
            @pl.when(p == s)
            def _():
                for o in owners:
                    scatter_copy(o).start()

        for k in range(CHUNKS):
            xy_send(0, k)

        @pl.when(s != 0)
        def _():
            choose_own(s)

        @pl.when(z != 0)
        def _():
            for t in (1, 2):
                ring_copy(t, 0).start()
                ring_copy(t, 1).start()
            core_copy(0, 0).start()

        @pl.when(s != 0)
        def _():
            choose_scattered(s)

        scatter(FAR[:8])

        @pl.when(root)
        def _():
            pb[s] = x_ref[...]

        @pl.when(s == 0)
        def _():
            loads[1].wait()
            loads[2].wait()

        order = (slot_col[s] == iota((N, DEPTH), 1).astype(F32)).astype(F32).astype(BF16)
        lower = split(li[s])
        lsh[...] = dot(lower[0], order).astype(BF16)
        lsl[...] = dot(lower[1], order).astype(BF16)
        uih[...], uil[...] = split(ui[s])

        def move(st, k):
            xy_arrive(st, k)
            xy_send(st + 1, k)

        chosen_t = pick_t[s].astype(BF16)[:, 0:FIX]
        is_target = jnp.sum(pick_t[s], axis=1, keepdims=True) > 0.5
        upper_inv = (uih[...], uil[...])
        trailing = q > s

        def from_core(t, side):
            @pl.when(chip(t, side) != 0)
            def _():
                core_copy(t, side, 1 - core).wait_recv()
                core_copy(t, side).wait_send()

        def gather_step(lo, hi, start=False):
            @pl.when(trailing)
            def _():
                term = product((lsh[:, lo:hi], lsl[:, lo:hi]), split(g_ref[s, lo:hi, :]))
                upp[...] = term if start else upp[...] + term

        def multiply(lo, hi):
            low[lo:hi, :] = product(split(pb[s, lo:hi, :]), upper_inv)

        def finish(lo, hi):
            @pl.when(p > s)
            def _():
                fixed = product(split(pf[s]), upper_inv)
                rows = jnp.where(is_target[lo:hi], select_rows(chosen_t[lo:hi], fixed), low[lo:hi, :])

                @pl.when(trailing)
                def _():
                    x_ref[lo:hi, :] = x_ref[lo:hi, :] - product(split(rows), split(upp[...]))

                @pl.when(root)
                def _():
                    x_ref[lo:hi, :] = rows

        move(0, 0)
        move(0, 1)
        scatter(FAR[8:])
        move(0, 2)
        move(1, 0)
        move(0, 3)
        ring_arrive(1)
        ring_arrive(2)
        move(1, 1)
        @pl.when(p >= HEADS)
        def _():
            scatter_copy(0).wait_recv()

        @pl.when(p < HEADS)
        def _():
            f_ref[s, 0:SLOT, :] = jnp.zeros((SLOT, N), F32)

        xy_send(0, CHUNKS)
        move(1, 2)
        move(0, CHUNKS)
        move(1, 3)
        move(1, CHUNKS)

        @pl.when(root)
        def _():
            pf[s] = f_ref[s]

        from_core(0, 0)
        for t in (1, 2):
            for side in range(2):
                from_core(t, side)
        gather_step(0, 256, True)
        xy_arrive(2, 0)
        xy_arrive(2, 1)
        multiply(0, CUT)
        ring_arrive(3)
        ring_arrive(4)
        for k in range(CHUNKS + 1):
            xy_sent(0, k)

        @pl.when(p > s)
        def _():
            x_ref[0:N, :] = jnp.where(is_target, select_rows(chosen_t, f_ref[s]), x_ref[0:N, :])

        for t in (3, 4):
            for side in range(2):
                from_core(t, side)
        gather_step(256, DEPTH)
        xy_arrive(2, 2)
        xy_arrive(2, 3)
        multiply(CUT, LONG)
        xy_arrive(2, CHUNKS)
        finish(0, N)

        @pl.when(jnp.logical_and(p == s, q <= s))
        def _():
            place = (slot_col[s] == iota((N, DEPTH), 1).astype(F32)).astype(F32).astype(BF16)
            x_ref[0:N, :] = select_rows(place, g_ref[s])

        @pl.when(jnp.logical_and(p == s, trailing))
        def _():
            x_ref[0:N, :] = upp[...]

        for k in range(CHUNKS + 1):
            for st in (1, 2):
                xy_sent(st, k)

        @pl.when(p == s)
        def _():
            for o in FAR:
                scatter_copy(o).wait_send()

        for side in range(2):
            for t in (1, 2, 3, 4):

                @pl.when(chip(0 if t < 3 else 2, side) != 0)
                def _(side=side, t=t):
                    ring_copy(t, side).wait_send()

        return carry

    lax.fori_loop(0, STEPS, stage, 0)
    for c in range(4):
        out_ref[pl.ds(c, N, stride=4), :] = x_ref[0:N, 128 * c : 128 * (c + 1)]


def body(matrix, pivots, lower_inv, upper_inv):
    vm, dma = pltpu.VMEM, pltpu.SemaphoreType.DMA
    any_space = pl.BlockSpec(memory_space=pl.ANY)
    done = pl.pallas_call(
        kernel,
        out_shape=jax.ShapeDtypeStruct((4 * N, 128), F32),
        in_specs=[any_space, pl.BlockSpec(memory_space=vm), any_space, any_space],
        out_specs=pl.BlockSpec(memory_space=vm),
        scratch_shapes=[
            vm((4 * N, 128), F32),
            vm((LONG, N), F32),
            vm((STEPS, N, N), F32),
            vm((STEPS, N, N), F32),
            vm((N, DEPTH), BF16),
            vm((N, DEPTH), BF16),
            vm((N, N), BF16),
            vm((N, N), BF16),
            vm((STEPS, SLOT, N), F32),
            vm((STEPS, N, 128), F32),
            vm((STEPS, 1, N), F32),
            vm((STEPS, N, 1), F32),
            vm((14 * SLOT, N), F32),
            vm((STEPS, FIX, N), F32),
            vm((STEPS, DEPTH, N), F32),
            vm((STEPS, LONG, N), F32),
            vm((STEPS, FIX, N), F32),
            vm((LONG, N), F32),
            vm((N, N), F32),
            dma((3,)),
            dma((18 * (CHUNKS + 1),)),
            dma((STEPS * 18 * (CHUNKS + 1),)),
            dma((8,)),
            dma((STEPS * 8,)),
            dma((9,)),
            dma((18,)),
            dma((14,)),
            dma((STEPS,)),
        ],
        compiler_params=pltpu.CompilerParams(
            collective_id=0, has_side_effects=True, vmem_limit_bytes=56 << 20
        ),
        cost_estimate=pl.CostEstimate(flops=10**10, bytes_accessed=7 << 20, transcendentals=0),
    )(matrix.reshape(4 * N, 128), pivots, lower_inv, upper_inv)
    return done.reshape(matrix.shape)


def solution(mesh):
    placed = (P(None, "prow", None, "pcol"), P(), P(), P())
    return jax.shard_map(
        body, mesh=mesh, in_specs=placed, out_specs=P(None, "prow", None, "pcol"), check_vma=False
    )
```

```python
import functools

import jax
import jax.numpy as jnp
from jax import lax
from jax.experimental import pallas as pl
from jax.experimental.pallas import tpu as pltpu
from jax.sharding import PartitionSpec as P

MESH = pl.DeviceIdType.MESH
F32 = jnp.float32
BF16 = jnp.bfloat16

N = 512
STEPS = 2
SLOT = 40
HEADS = 2
DEPTH = 640
FIX = 48
SIZES = (24, 24, 24, 16, 8)
CHUNKS = len(SIZES) - 1
LONG = 6 * sum(SIZES[:-1])
CUT = 6 * sum(SIZES[:2])
SUB = ((0, 24), (24, 16))
FAR = (6, 7, 4, 5, 8, 9, 2, 3, 10, 11, 0, 1, 12, 13)


def dot(a, b):
    return jnp.dot(a, b, preferred_element_type=F32)


def split(v):
    high = v.astype(BF16)
    return high, (v - high.astype(F32)).astype(BF16)


def product(a, b):
    return dot(a[0], b[0]) + (dot(a[0], b[1]) + dot(a[1], b[0]))


def select_rows(chooser, v):
    high = v.astype(BF16)
    rest = v - high.astype(F32)
    mid = rest.astype(BF16)
    low = (rest - mid.astype(F32)).astype(BF16)
    return dot(chooser, high) + (dot(chooser, mid) + dot(chooser, low))


def iota(shape, dim):
    return lax.broadcasted_iota(jnp.int32, shape, dim)


def kernel(
    lin_hbm, piv_ref, linv_hbm, uinv_hbm, out_ref,
    lin, x_ref, li, ui, lsh, lsl, uih, uil, pick, pick_t, slot_row, slot_col,
    pack, f_ref, g_ref, pb, pf, low, upp,
    load_sem, xs, xr, rs, rr, bs, br, ss, sr,
):
    p = lax.axis_index("prow")
    q = lax.axis_index("pcol")
    z, core = p // 2, p % 2
    y, x = q // 4, q % 4
    along_z = [lax.rem(z + d, 8) * 2 + core for d in (1, 7, 2, 6)]
    sibling = z * 2 + (1 - core)

    def at_x(d):
        return (p, y * 4 + lax.rem(x + d, 4))

    def at_y(d):
        return (p, lax.rem(y + d, 4) * 4 + x)

    barrier = pltpu.get_barrier_semaphore()
    friends = [at_x(1), at_x(2), at_x(3), at_y(1), at_y(2), at_y(3), (sibling, q)]
    friends += [(other, q) for other in along_z]

    @pl.when(p >= HEADS)
    def _():
        for head in range(HEADS):
            pl.semaphore_signal(barrier, inc=1, device_id=(head, q), device_id_type=MESH)

    for friend in friends:
        pl.semaphore_signal(barrier, inc=1, device_id=friend, device_id_type=MESH)

    loads = [
        pltpu.make_async_copy(lin_hbm, lin, load_sem.at[0]),
        pltpu.make_async_copy(linv_hbm, li, load_sem.at[1]),
        pltpu.make_async_copy(uinv_hbm, ui, load_sem.at[2]),
    ]
    for load in loads:
        load.start()

    before = (iota((N, N), 0) < iota((N, N), 1)).astype(BF16)
    same = iota((N, N), 0) == iota((N, N), 1)
    first = (p - HEADS) * SLOT
    empty = jnp.where(z == 0, 0, jnp.where(z < 4, 2 * z - 1, jnp.where(z == 4, 7, 2 * (8 - z))))
    for s in range(STEPS):
        piv = piv_ref[s : s + 1, :]
        owner = lax.shift_right_logical(piv, 9)
        place = jnp.bitwise_and(piv, N - 1)
        owned = (iota((16, N), 0) == owner).astype(F32)
        rank = jnp.sum(owned * dot(owned.astype(BF16), before), axis=0, keepdims=True)
        slots = ((owner - HEADS) * SLOT).astype(F32) + rank
        back = jnp.bitwise_and(z - lax.shift_right_logical(owner, 1), 7)
        turn = jnp.where(back == 0, 0, jnp.where(back < 4, 2 * back - 1, jnp.where(back == 4, 7, 2 * (8 - back))))
        gathered = (turn * (2 * SLOT) + jnp.bitwise_and(owner, 1) * SLOT).astype(F32) + rank
        slots_down = jnp.sum(jnp.where(same, slots, 0.0), axis=1, keepdims=True)
        place_down = jnp.sum(jnp.where(same, place.astype(F32), 0.0), axis=1, keepdims=True)
        slot_row[s] = slots
        slot_col[s] = jnp.sum(jnp.where(same, gathered, 0.0), axis=1, keepdims=True)
        mine = (slots == (iota((48, N), 0) + first).astype(F32)).astype(BF16)
        pick[s] = dot(mine, (place_down == iota((N, N), 1).astype(F32)).astype(BF16))[:SLOT]
        across = iota((N, 128), 1)
        mine_t = jnp.logical_and(slots_down == (across + first).astype(F32), across < SLOT)
        pick_t[s] = dot((place.astype(F32) == iota((N, N), 0).astype(F32)).astype(BF16), mine_t.astype(F32).astype(BF16))
        f_ref[s, SLOT:FIX, :] = jnp.zeros((FIX - SLOT, N), F32)
        g_ref[s, pl.ds(pl.multiple_of(empty * 2 * SLOT, 8), 2 * SLOT), :] = jnp.zeros((2 * SLOT, N), F32)

    x_ref[N:LONG, :] = jnp.zeros((LONG - N, N), F32)
    loads[0].wait()
    for c in range(4):
        x_ref[0:N, 128 * c : 128 * (c + 1)] = lin[pl.ds(c, N, stride=4), :]

    own_rows = pl.ds(pl.multiple_of(core * SLOT, 8), SLOT)

    def choose_own(s):
        @pl.when(z != 0)
        def _():
            g_ref[s, own_rows, :] = select_rows(pick[s].astype(BF16), x_ref[0:N, :])

    def choose_scattered(s):
        @pl.when(p == s)
        def _():
            chooser = (slot_row[s] == iota((14 * SLOT, N), 0).astype(F32)).astype(F32).astype(BF16)
            pack[...] = select_rows(chooser, x_ref[0:N, :])

    choose_own(0)
    choose_scattered(0)

    @pl.when(p >= HEADS)
    def _():
        pl.semaphore_wait(barrier, len(friends))

    @pl.when(p < HEADS)
    def _():
        pl.semaphore_wait(barrier, len(friends) + 14)

    def remote(src, dst, send, recv, device):
        return pltpu.make_async_remote_copy(
            src_ref=src, dst_ref=dst, send_sem=send, recv_sem=recv, device_id=device, device_id_type=MESH
        )

    def stage(s, carry):
        offs = (lax.rem(x - s + 4, 4), y)
        below = p > s
        root = jnp.logical_and(q == s, below)

        def rows_of(k, h, d):
            at = 6 * sum(SIZES[:k]) if k < CHUNKS else 0
            return pl.ds(pl.multiple_of(at + (h * 3 + d - 1) * SIZES[k], 8), SIZES[k])

        def target(k):
            return pb.at[s] if k < CHUNKS else pf.at[s]

        def source(k):
            return x_ref if k < CHUNKS else f_ref.at[s]

        def index(st, k, h, d):
            return ((st * (CHUNKS + 1) + k) * 2 + h) * 3 + d - 1

        def xy_copy(st, k, h, d, piece, arrival):
            device = at_x(d) if (h == 0) == (st != 1) else at_y(d)
            rows = rows_of(k, h, piece)
            src = source(k).at[rows] if st == 0 else target(k).at[rows]
            return remote(
                src, target(k).at[rows], xs.at[index(st, k, h, d)],
                xr.at[s * 6 * 3 * (CHUNKS + 1) + index(st, k, h, arrival)], device,
            )

        def each_send(st, k, action):
            for h in range(2):
                mine, other = offs[h], offs[1 - h]
                if st == 0:

                    @pl.when(root)
                    def _(h=h):
                        for d in (1, 2, 3):
                            action(xy_copy(0, k, h, d, d, 1))

                elif st == 1:

                    @pl.when(jnp.logical_and(below, jnp.logical_and(other == 0, mine != 0)))
                    def _(h=h, mine=mine):
                        for d in (1, 2, 3):
                            action(xy_copy(1, k, h, d, mine, 1))

                else:
                    for d in (1, 2, 3):
                        spared = jnp.logical_and(other == 0, lax.rem(mine + d, 4) == 0)

                        @pl.when(jnp.logical_and(below, jnp.logical_and(mine != 0, jnp.logical_not(spared))))
                        def _(h=h, mine=mine, d=d):
                            action(xy_copy(2, k, h, d, mine, d))

        def xy_send(st, k):
            each_send(st, k, lambda copy: copy.start())

        def xy_sent(st, k):
            each_send(st, k, lambda copy: copy.wait_send())

        def xy_arrive(st, k):
            for h in range(2):
                mine, other = offs[h], offs[1 - h]
                if st == 0:

                    @pl.when(jnp.logical_and(below, jnp.logical_and(other == 0, mine != 0)))
                    def _(h=h, mine=mine):
                        xy_copy(0, k, h, 1, mine, 1).wait_recv()

                elif st == 1:

                    @pl.when(jnp.logical_and(below, jnp.logical_and(other != 0, mine != 0)))
                    def _(h=h, mine=mine):
                        xy_copy(1, k, h, 1, mine, 1).wait_recv()

                else:
                    for d in (1, 2, 3):
                        giver = lax.rem(mine + 4 - d, 4)

                        @pl.when(jnp.logical_and(below, jnp.logical_and(giver != 0, jnp.logical_not(root))))
                        def _(h=h, d=d, giver=giver):
                            xy_copy(2, k, h, d, giver, d).wait_recv()

        def chip(t, side):
            return lax.rem(z + (8 - t if side == 0 else t), 8)

        def block(t, side, c, part):
            turn = 0 if t == 0 else (7 if t == 4 else 2 * t - 1 + side)
            return g_ref.at[s, pl.ds(pl.multiple_of(turn * 2 * SLOT + c * SLOT + part[0], 8), part[1])]

        def ring_copy(t, side):
            n = side * 4 + t - 1
            part = SUB[side] if t == 4 else (0, SLOT)
            return remote(
                block(0 if t < 3 else 2, side, core, part), block(t, side, core, part),
                rs.at[n], rr.at[s * 8 + n], (along_z[side if t % 2 else 2 + side], q),
            )

        def core_copy(t, side, c=core):
            ref = block(t, side, c, SUB[side] if t == 4 else (0, SLOT))
            n = 0 if t == 0 else 1 + side * 4 + t - 1
            return remote(ref, ref, bs.at[n], br.at[s * 9 + n], (sibling, q))

        trailing = q > s

        def either(everywhere, toward):
            return jnp.logical_or(
                jnp.logical_and(trailing, everywhere), jnp.logical_and(jnp.logical_not(trailing), toward)
            )

        def sends(t, side):
            ahead = lax.rem(8 - z, 8) if side == 0 else z
            toward = {1: ahead == 1, 2: jnp.logical_and(ahead >= 2, ahead <= 4), 3: ahead == 1, 4: ahead == 2}[t]
            return either(chip(0 if t < 3 else 2, side) != 0, toward)

        def receives(t, side):
            ahead = lax.rem(8 - z, 8) if side == 0 else z
            return either(chip(t, side) != 0, ahead <= 2 if t == 2 else ahead == 0)

        def shares(t, side):
            if t == 0:
                return jnp.logical_and(trailing, z != 0)
            return either(chip(t, side) != 0, z == 0)

        def ring_start(t, side):
            @pl.when(sends(t, side))
            def _():
                ring_copy(t, side).start()

        def ring_arrive(t):
            for side in range(2):

                @pl.when(receives(t, side))
                def _(side=side):
                    ring_copy(t, side).wait_recv()

                if t == 2:
                    ring_start(3, side)
                    ring_start(4, side)

                @pl.when(shares(t, side))
                def _(side=side):
                    core_copy(t, side).start()

        def scatter_copy(o):
            rows = pl.ds(o * SLOT, SLOT)
            return remote(pack.at[rows], f_ref.at[s, pl.ds(0, SLOT)], ss.at[o], sr.at[s], (o + HEADS, q))

        def scatter(owners):
            @pl.when(p == s)
            def _():
                for o in owners:
                    scatter_copy(o).start()

        for k in range(CHUNKS):
            xy_send(0, k)

        @pl.when(s != 0)
        def _():
            choose_own(s)

        for t in (1, 2):
            for side in range(2):
                ring_start(t, side)

        @pl.when(shares(0, 0))
        def _():
            core_copy(0, 0).start()

        @pl.when(s != 0)
        def _():
            choose_scattered(s)

        scatter(FAR[:8])

        @pl.when(root)
        def _():
            pb[s] = x_ref[...]

        @pl.when(s == 0)
        def _():
            loads[1].wait()
            loads[2].wait()

        order = (slot_col[s] == iota((N, DEPTH), 1).astype(F32)).astype(F32).astype(BF16)
        lower = split(li[s])
        lsh[...] = dot(lower[0], order).astype(BF16)
        lsl[...] = dot(lower[1], order).astype(BF16)
        uih[...], uil[...] = split(ui[s])

        def move(st, k):
            xy_arrive(st, k)
            xy_send(st + 1, k)

        chosen_t = pick_t[s].astype(BF16)[:, 0:FIX]
        is_target = jnp.sum(pick_t[s], axis=1, keepdims=True) > 0.5
        upper_inv = (uih[...], uil[...])

        def from_core(t, side):
            @pl.when(shares(t, side))
            def _():
                core_copy(t, side, 1 - core).wait_recv()
                core_copy(t, side).wait_send()

        def gather_step(lo, hi, start=False):
            @pl.when(trailing)
            def _():
                term = product((lsh[:, lo:hi], lsl[:, lo:hi]), split(g_ref[s, lo:hi, :]))
                upp[...] = term if start else upp[...] + term

        def multiply(lo, hi):
            @pl.when(below)
            def _():
                low[lo:hi, :] = product(split(pb[s, lo:hi, :]), upper_inv)

        def finish(lo, hi):
            @pl.when(jnp.logical_and(below, trailing))
            def _():
                x_ref[lo:hi, :] = x_ref[lo:hi, :] - product(split(low[lo:hi, :]), split(upp[...]))

            @pl.when(root)
            def _():
                x_ref[lo:hi, :] = low[lo:hi, :]

        def swap_in():
            @pl.when(jnp.logical_and(below, q >= s))
            def _():
                fixed = product(split(pf[s]), upper_inv)

                @pl.when(root)
                def _():
                    f_ref[s] = fixed

                @pl.when(trailing)
                def _():
                    f_ref[s] = f_ref[s] - product(split(fixed), split(upp[...]))

            @pl.when(below)
            def _():
                x_ref[0:N, :] = jnp.where(is_target, select_rows(chosen_t, f_ref[s]), x_ref[0:N, :])

        scatter(FAR[8:])
        move(0, 0)
        move(0, 1)
        move(0, 2)
        move(1, 0)
        move(0, 3)
        ring_arrive(1)
        ring_arrive(2)
        @pl.when(p < HEADS)
        def _():
            f_ref[s, 0:SLOT, :] = jnp.zeros((SLOT, N), F32)

        @pl.when(jnp.logical_and(p >= HEADS, root))
        def _():
            scatter_copy(0).wait_recv()

        xy_send(0, CHUNKS)
        move(1, 1)
        move(0, CHUNKS)
        move(1, 2)
        move(1, 3)
        move(1, CHUNKS)

        @pl.when(root)
        def _():
            pf[s] = f_ref[s]

        from_core(0, 0)
        for t in (1, 2):
            for side in range(2):
                from_core(t, side)
        gather_step(0, 256, True)
        xy_arrive(2, 0)
        xy_arrive(2, 1)
        multiply(0, CUT)
        ring_arrive(3)
        ring_arrive(4)
        for k in range(CHUNKS + 1):
            xy_sent(0, k)

        for t in (3, 4):
            for side in range(2):
                from_core(t, side)
        gather_step(256, DEPTH)
        finish(0, CUT)
        xy_arrive(2, 2)
        xy_arrive(2, 3)
        multiply(CUT, LONG)
        finish(CUT, N)
        xy_arrive(2, CHUNKS)

        @pl.when(jnp.logical_and(p >= HEADS, jnp.logical_not(root)))
        def _():
            scatter_copy(0).wait_recv()

        swap_in()

        @pl.when(jnp.logical_and(p == s, q <= s))
        def _():
            place = (slot_col[s] == iota((N, DEPTH), 1).astype(F32)).astype(F32).astype(BF16)
            x_ref[0:N, :] = select_rows(place, g_ref[s])

        @pl.when(jnp.logical_and(p == s, trailing))
        def _():
            x_ref[0:N, :] = upp[...]

        for k in range(CHUNKS + 1):
            for st in (1, 2):
                xy_sent(st, k)

        @pl.when(p == s)
        def _():
            for o in FAR:
                scatter_copy(o).wait_send()

        for side in range(2):
            for t in (1, 2, 3, 4):

                @pl.when(sends(t, side))
                def _(side=side, t=t):
                    ring_copy(t, side).wait_send()

        return carry

    lax.fori_loop(0, STEPS, stage, 0)
    for c in range(4):
        out_ref[pl.ds(c, N, stride=4), :] = x_ref[0:N, 128 * c : 128 * (c + 1)]


def body(matrix, pivots, lower_inv, upper_inv):
    vm, dma = pltpu.VMEM, pltpu.SemaphoreType.DMA
    any_space = pl.BlockSpec(memory_space=pl.ANY)
    done = pl.pallas_call(
        kernel,
        out_shape=jax.ShapeDtypeStruct((4 * N, 128), F32),
        in_specs=[any_space, pl.BlockSpec(memory_space=vm), any_space, any_space],
        out_specs=pl.BlockSpec(memory_space=vm),
        scratch_shapes=[
            vm((4 * N, 128), F32),
            vm((LONG, N), F32),
            vm((STEPS, N, N), F32),
            vm((STEPS, N, N), F32),
            vm((N, DEPTH), BF16),
            vm((N, DEPTH), BF16),
            vm((N, N), BF16),
            vm((N, N), BF16),
            vm((STEPS, SLOT, N), F32),
            vm((STEPS, N, 128), F32),
            vm((STEPS, 1, N), F32),
            vm((STEPS, N, 1), F32),
            vm((14 * SLOT, N), F32),
            vm((STEPS, FIX, N), F32),
            vm((STEPS, DEPTH, N), F32),
            vm((STEPS, LONG, N), F32),
            vm((STEPS, FIX, N), F32),
            vm((LONG, N), F32),
            vm((N, N), F32),
            dma((3,)),
            dma((18 * (CHUNKS + 1),)),
            dma((STEPS * 18 * (CHUNKS + 1),)),
            dma((8,)),
            dma((STEPS * 8,)),
            dma((9,)),
            dma((18,)),
            dma((14,)),
            dma((STEPS,)),
        ],
        compiler_params=pltpu.CompilerParams(
            collective_id=0, has_side_effects=True, vmem_limit_bytes=56 << 20
        ),
        cost_estimate=pl.CostEstimate(flops=10**10, bytes_accessed=7 << 20, transcendentals=0),
    )(matrix.reshape(4 * N, 128), pivots, lower_inv, upper_inv)
    return done.reshape(matrix.shape)


def solution(mesh):
    placed = (P(None, "prow", None, "pcol"), P(), P(), P())
    return jax.shard_map(
        body, mesh=mesh, in_specs=placed, out_specs=P(None, "prow", None, "pcol"), check_vma=False
    )
```

```python
import functools

import jax
import jax.numpy as jnp
from jax import lax
from jax.experimental import pallas as pl
from jax.experimental.pallas import tpu as pltpu
from jax.sharding import PartitionSpec as P

MESH = pl.DeviceIdType.MESH
F32 = jnp.float32
BF16 = jnp.bfloat16

N = 512
STEPS = 2
SLOT = 40
HEADS = 2
DEPTH = 640
FIX = 48
SIZES = (24, 24, 24, 16, 8)
CHUNKS = len(SIZES) - 1
LONG = 6 * sum(SIZES[:-1])
CUT = 6 * sum(SIZES[:2])
SUB = ((0, 24), (24, 16))
FAR = (6, 7, 4, 5, 8, 9, 2, 3, 10, 11, 0, 1, 12, 13)


def dot(a, b):
    return jnp.dot(a, b, preferred_element_type=F32)


def split(v):
    high = v.astype(BF16)
    return high, (v - high.astype(F32)).astype(BF16)


def product(a, b):
    return dot(a[0], b[0]) + (dot(a[0], b[1]) + dot(a[1], b[0]))


def select_rows(chooser, v):
    high = v.astype(BF16)
    rest = v - high.astype(F32)
    mid = rest.astype(BF16)
    low = (rest - mid.astype(F32)).astype(BF16)
    return dot(chooser, high) + (dot(chooser, mid) + dot(chooser, low))


def iota(shape, dim):
    return lax.broadcasted_iota(jnp.int32, shape, dim)


def kernel(
    lin_hbm, piv_ref, linv_hbm, uinv_hbm, out_ref,
    lin, x_ref, li, ui, lsh, lsl, uih, uil, pick, pick_t, slot_row, slot_col,
    pack, f_ref, g_ref, pb, pf, low, upp,
    load_sem, xs, xr, rs, rr, bs, br, ss, sr,
):
    p = lax.axis_index("prow")
    q = lax.axis_index("pcol")
    z, core = p // 2, p % 2
    y, x = q // 4, q % 4
    along_z = [lax.rem(z + d, 8) * 2 + core for d in (1, 7, 2, 6)]
    sibling = z * 2 + (1 - core)

    def at_x(d):
        return (p, y * 4 + lax.rem(x + d, 4))

    def at_y(d):
        return (p, lax.rem(y + d, 4) * 4 + x)

    barrier = pltpu.get_barrier_semaphore()
    friends = [at_x(1), at_x(2), at_x(3), at_y(1), at_y(2), at_y(3), (sibling, q)]
    friends += [(other, q) for other in along_z]

    @pl.when(p >= HEADS)
    def _():
        for head in range(HEADS):
            pl.semaphore_signal(barrier, inc=1, device_id=(head, q), device_id_type=MESH)

    for friend in friends:
        pl.semaphore_signal(barrier, inc=1, device_id=friend, device_id_type=MESH)

    loads = [
        pltpu.make_async_copy(lin_hbm, lin, load_sem.at[0]),
        pltpu.make_async_copy(linv_hbm, li, load_sem.at[1]),
        pltpu.make_async_copy(uinv_hbm, ui, load_sem.at[2]),
    ]
    for load in loads:
        load.start()

    before = (iota((N, N), 0) < iota((N, N), 1)).astype(BF16)
    same = iota((N, N), 0) == iota((N, N), 1)
    first = (p - HEADS) * SLOT
    empty = jnp.where(z == 0, 0, jnp.where(z < 4, 2 * z - 1, jnp.where(z == 4, 7, 2 * (8 - z))))
    for s in range(STEPS):
        piv = piv_ref[s : s + 1, :]
        owner = lax.shift_right_logical(piv, 9)
        place = jnp.bitwise_and(piv, N - 1)
        owned = (iota((16, N), 0) == owner).astype(F32)
        rank = jnp.sum(owned * dot(owned.astype(BF16), before), axis=0, keepdims=True)
        slots = ((owner - HEADS) * SLOT).astype(F32) + rank
        back = jnp.bitwise_and(z - lax.shift_right_logical(owner, 1), 7)
        turn = jnp.where(back == 0, 0, jnp.where(back < 4, 2 * back - 1, jnp.where(back == 4, 7, 2 * (8 - back))))
        gathered = (turn * (2 * SLOT) + jnp.bitwise_and(owner, 1) * SLOT).astype(F32) + rank
        slots_down = jnp.sum(jnp.where(same, slots, 0.0), axis=1, keepdims=True)
        place_down = jnp.sum(jnp.where(same, place.astype(F32), 0.0), axis=1, keepdims=True)
        slot_row[s] = slots
        slot_col[s] = jnp.sum(jnp.where(same, gathered, 0.0), axis=1, keepdims=True)
        mine = (slots == (iota((48, N), 0) + first).astype(F32)).astype(BF16)
        pick[s] = dot(mine, (place_down == iota((N, N), 1).astype(F32)).astype(BF16))[:SLOT]
        across = iota((N, 128), 1)
        mine_t = jnp.logical_and(slots_down == (across + first).astype(F32), across < SLOT)
        pick_t[s] = dot((place.astype(F32) == iota((N, N), 0).astype(F32)).astype(BF16), mine_t.astype(F32).astype(BF16))
        f_ref[s, SLOT:FIX, :] = jnp.zeros((FIX - SLOT, N), F32)
        g_ref[s, pl.ds(pl.multiple_of(empty * 2 * SLOT, 8), 2 * SLOT), :] = jnp.zeros((2 * SLOT, N), F32)

    x_ref[N:LONG, :] = jnp.zeros((LONG - N, N), F32)
    loads[0].wait()
    for c in range(4):
        x_ref[0:N, 128 * c : 128 * (c + 1)] = lin[pl.ds(c, N, stride=4), :]

    own_rows = pl.ds(pl.multiple_of(core * SLOT, 8), SLOT)

    def choose_own(s):
        @pl.when(z != 0)
        def _():
            g_ref[s, own_rows, :] = select_rows(pick[s].astype(BF16), x_ref[0:N, :])

    def choose_scattered(s):
        @pl.when(p == s)
        def _():
            chooser = (slot_row[s] == iota((14 * SLOT, N), 0).astype(F32)).astype(F32).astype(BF16)
            pack[...] = select_rows(chooser, x_ref[0:N, :])

    choose_own(0)
    choose_scattered(0)

    @pl.when(p >= HEADS)
    def _():
        pl.semaphore_wait(barrier, len(friends))

    @pl.when(p < HEADS)
    def _():
        pl.semaphore_wait(barrier, len(friends) + 14)

    def remote(src, dst, send, recv, device):
        return pltpu.make_async_remote_copy(
            src_ref=src, dst_ref=dst, send_sem=send, recv_sem=recv, device_id=device, device_id_type=MESH
        )

    def stage(s, carry):
        offs = (lax.rem(x - s + 4, 4), y)
        below = p > s
        root = jnp.logical_and(q == s, below)

        def rows_of(k, h, d):
            at = 6 * sum(SIZES[:k]) if k < CHUNKS else 0
            return pl.ds(pl.multiple_of(at + (h * 3 + d - 1) * SIZES[k], 8), SIZES[k])

        def target(k):
            return pb.at[s] if k < CHUNKS else pf.at[s]

        def source(k):
            return x_ref if k < CHUNKS else f_ref.at[s]

        def index(st, k, h, d):
            return ((st * (CHUNKS + 1) + k) * 2 + h) * 3 + d - 1

        def xy_copy(st, k, h, d, piece, arrival):
            device = at_x(d) if (h == 0) == (st != 1) else at_y(d)
            rows = rows_of(k, h, piece)
            src = source(k).at[rows] if st == 0 else target(k).at[rows]
            return remote(
                src, target(k).at[rows], xs.at[index(st, k, h, d)],
                xr.at[s * 6 * 3 * (CHUNKS + 1) + index(st, k, h, arrival)], device,
            )

        def each_send(st, k, action):
            for h in range(2):
                mine, other = offs[h], offs[1 - h]
                if st == 0:

                    @pl.when(root)
                    def _(h=h):
                        for d in (1, 2, 3):
                            action(xy_copy(0, k, h, d, d, 1))

                elif st == 1:

                    @pl.when(jnp.logical_and(below, jnp.logical_and(other == 0, mine != 0)))
                    def _(h=h, mine=mine):
                        for d in (1, 2, 3):
                            action(xy_copy(1, k, h, d, mine, 1))

                else:
                    for d in (1, 2, 3):
                        spared = jnp.logical_and(other == 0, lax.rem(mine + d, 4) == 0)

                        @pl.when(jnp.logical_and(below, jnp.logical_and(mine != 0, jnp.logical_not(spared))))
                        def _(h=h, mine=mine, d=d):
                            action(xy_copy(2, k, h, d, mine, d))

        def xy_send(st, k):
            each_send(st, k, lambda copy: copy.start())

        def xy_sent(st, k):
            each_send(st, k, lambda copy: copy.wait_send())

        def xy_arrive(st, k):
            for h in range(2):
                mine, other = offs[h], offs[1 - h]
                if st == 0:

                    @pl.when(jnp.logical_and(below, jnp.logical_and(other == 0, mine != 0)))
                    def _(h=h, mine=mine):
                        xy_copy(0, k, h, 1, mine, 1).wait_recv()

                elif st == 1:

                    @pl.when(jnp.logical_and(below, jnp.logical_and(other != 0, mine != 0)))
                    def _(h=h, mine=mine):
                        xy_copy(1, k, h, 1, mine, 1).wait_recv()

                else:
                    for d in (1, 2, 3):
                        giver = lax.rem(mine + 4 - d, 4)

                        @pl.when(jnp.logical_and(below, jnp.logical_and(giver != 0, jnp.logical_not(root))))
                        def _(h=h, d=d, giver=giver):
                            xy_copy(2, k, h, d, giver, d).wait_recv()

        def chip(t, side):
            return lax.rem(z + (8 - t if side == 0 else t), 8)

        def block(t, side, c, part):
            turn = 0 if t == 0 else (7 if t == 4 else 2 * t - 1 + side)
            return g_ref.at[s, pl.ds(pl.multiple_of(turn * 2 * SLOT + c * SLOT + part[0], 8), part[1])]

        def ring_copy(t, side):
            n = side * 4 + t - 1
            part = SUB[side] if t == 4 else (0, SLOT)
            return remote(
                block(0 if t < 3 else 2, side, core, part), block(t, side, core, part),
                rs.at[n], rr.at[s * 8 + n], (along_z[side if t % 2 else 2 + side], q),
            )

        def core_copy(t, side, c=core):
            ref = block(t, side, c, SUB[side] if t == 4 else (0, SLOT))
            n = 0 if t == 0 else 1 + side * 4 + t - 1
            return remote(ref, ref, bs.at[n], br.at[s * 9 + n], (sibling, q))

        trailing = q > s

        def either(everywhere, toward):
            return jnp.logical_or(
                jnp.logical_and(trailing, everywhere), jnp.logical_and(jnp.logical_not(trailing), toward)
            )

        def sends(t, side):
            ahead = lax.rem(8 - z, 8) if side == 0 else z
            toward = {1: ahead == 1, 2: jnp.logical_and(ahead >= 2, ahead <= 4), 3: ahead == 1, 4: ahead == 2}[t]
            return either(chip(0 if t < 3 else 2, side) != 0, toward)

        def receives(t, side):
            ahead = lax.rem(8 - z, 8) if side == 0 else z
            return either(chip(t, side) != 0, ahead <= 2 if t == 2 else ahead == 0)

        def shares(t, side):
            if t == 0:
                return jnp.logical_and(trailing, z != 0)
            return either(chip(t, side) != 0, z == 0)

        def ring_start(t, side):
            @pl.when(sends(t, side))
            def _():
                ring_copy(t, side).start()

        def ring_arrive(t):
            for side in range(2):

                @pl.when(receives(t, side))
                def _(side=side):
                    ring_copy(t, side).wait_recv()

                if t == 2:
                    ring_start(3, side)
                    ring_start(4, side)

                @pl.when(shares(t, side))
                def _(side=side):
                    core_copy(t, side).start()

        def scatter_copy(o):
            rows = pl.ds(o * SLOT, SLOT)
            return remote(pack.at[rows], f_ref.at[s, pl.ds(0, SLOT)], ss.at[o], sr.at[s], (o + HEADS, q))

        def scatter(owners):
            @pl.when(p == s)
            def _():
                for o in owners:
                    scatter_copy(o).start()

        for k in range(CHUNKS):
            xy_send(0, k)

        @pl.when(s != 0)
        def _():
            choose_own(s)

        for t in (2, 1):
            for side in range(2):
                ring_start(t, side)

        @pl.when(shares(0, 0))
        def _():
            core_copy(0, 0).start()

        @pl.when(s != 0)
        def _():
            choose_scattered(s)

        scatter(FAR[:8])

        @pl.when(root)
        def _():
            pb[s] = x_ref[...]

        @pl.when(s == 0)
        def _():
            loads[1].wait()
            loads[2].wait()

        order = (slot_col[s] == iota((N, DEPTH), 1).astype(F32)).astype(F32).astype(BF16)
        lower = split(li[s])
        lsh[...] = dot(lower[0], order).astype(BF16)
        lsl[...] = dot(lower[1], order).astype(BF16)
        uih[...], uil[...] = split(ui[s])

        def move(st, k):
            xy_arrive(st, k)
            xy_send(st + 1, k)

        chosen_t = pick_t[s].astype(BF16)[:, 0:FIX]
        is_target = jnp.sum(pick_t[s], axis=1, keepdims=True) > 0.5
        upper_inv = (uih[...], uil[...])

        def from_core(t, side):
            @pl.when(shares(t, side))
            def _():
                core_copy(t, side, 1 - core).wait_recv()
                core_copy(t, side).wait_send()

        def gather_step(lo, hi, start=False):
            @pl.when(trailing)
            def _():
                term = product((lsh[:, lo:hi], lsl[:, lo:hi]), split(g_ref[s, lo:hi, :]))
                upp[...] = term if start else upp[...] + term

        def multiply(lo, hi):
            @pl.when(below)
            def _():
                low[lo:hi, :] = product(split(pb[s, lo:hi, :]), upper_inv)

        def finish(lo, hi):
            @pl.when(jnp.logical_and(below, trailing))
            def _():
                x_ref[lo:hi, :] = x_ref[lo:hi, :] - product(split(low[lo:hi, :]), split(upp[...]))

            @pl.when(root)
            def _():
                x_ref[lo:hi, :] = low[lo:hi, :]

        def swap_in():
            @pl.when(jnp.logical_and(below, q >= s))
            def _():
                fixed = product(split(pf[s]), upper_inv)

                @pl.when(root)
                def _():
                    f_ref[s] = fixed

                @pl.when(trailing)
                def _():
                    f_ref[s] = f_ref[s] - product(split(fixed), split(upp[...]))

            @pl.when(below)
            def _():
                x_ref[0:N, :] = jnp.where(is_target, select_rows(chosen_t, f_ref[s]), x_ref[0:N, :])

        scatter(FAR[8:])
        move(0, 0)
        move(0, 1)
        move(0, 2)
        move(1, 0)
        move(0, 3)
        ring_arrive(2)
        ring_arrive(1)
        @pl.when(p < HEADS)
        def _():
            f_ref[s, 0:SLOT, :] = jnp.zeros((SLOT, N), F32)

        @pl.when(jnp.logical_and(p >= HEADS, root))
        def _():
            scatter_copy(0).wait_recv()

        xy_send(0, CHUNKS)
        move(1, 1)
        move(0, CHUNKS)
        move(1, 2)
        move(1, 3)
        move(1, CHUNKS)

        @pl.when(root)
        def _():
            pf[s] = f_ref[s]

        from_core(0, 0)
        for t in (1, 2):
            for side in range(2):
                from_core(t, side)
        gather_step(0, 256, True)
        xy_arrive(2, 0)
        xy_arrive(2, 1)
        multiply(0, CUT)
        ring_arrive(3)
        ring_arrive(4)
        for k in range(CHUNKS + 1):
            xy_sent(0, k)

        for t in (3, 4):
            for side in range(2):
                from_core(t, side)
        gather_step(256, DEPTH)
        finish(0, CUT)
        xy_arrive(2, 2)
        xy_arrive(2, 3)
        multiply(CUT, LONG)
        finish(CUT, N)
        xy_arrive(2, CHUNKS)

        @pl.when(jnp.logical_and(p >= HEADS, jnp.logical_not(root)))
        def _():
            scatter_copy(0).wait_recv()

        swap_in()

        @pl.when(jnp.logical_and(p == s, q <= s))
        def _():
            place = (slot_col[s] == iota((N, DEPTH), 1).astype(F32)).astype(F32).astype(BF16)
            x_ref[0:N, :] = select_rows(place, g_ref[s])

        @pl.when(jnp.logical_and(p == s, trailing))
        def _():
            x_ref[0:N, :] = upp[...]

        for k in range(CHUNKS + 1):
            for st in (1, 2):
                xy_sent(st, k)

        @pl.when(p == s)
        def _():
            for o in FAR:
                scatter_copy(o).wait_send()

        for side in range(2):
            for t in (1, 2, 3, 4):

                @pl.when(sends(t, side))
                def _(side=side, t=t):
                    ring_copy(t, side).wait_send()

        return carry

    lax.fori_loop(0, STEPS, stage, 0)
    for c in range(4):
        out_ref[pl.ds(c, N, stride=4), :] = x_ref[0:N, 128 * c : 128 * (c + 1)]


def body(matrix, pivots, lower_inv, upper_inv):
    vm, dma = pltpu.VMEM, pltpu.SemaphoreType.DMA
    any_space = pl.BlockSpec(memory_space=pl.ANY)
    done = pl.pallas_call(
        kernel,
        out_shape=jax.ShapeDtypeStruct((4 * N, 128), F32),
        in_specs=[any_space, pl.BlockSpec(memory_space=vm), any_space, any_space],
        out_specs=pl.BlockSpec(memory_space=vm),
        scratch_shapes=[
            vm((4 * N, 128), F32),
            vm((LONG, N), F32),
            vm((STEPS, N, N), F32),
            vm((STEPS, N, N), F32),
            vm((N, DEPTH), BF16),
            vm((N, DEPTH), BF16),
            vm((N, N), BF16),
            vm((N, N), BF16),
            vm((STEPS, SLOT, N), F32),
            vm((STEPS, N, 128), F32),
            vm((STEPS, 1, N), F32),
            vm((STEPS, N, 1), F32),
            vm((14 * SLOT, N), F32),
            vm((STEPS, FIX, N), F32),
            vm((STEPS, DEPTH, N), F32),
            vm((STEPS, LONG, N), F32),
            vm((STEPS, FIX, N), F32),
            vm((LONG, N), F32),
            vm((N, N), F32),
            dma((3,)),
            dma((18 * (CHUNKS + 1),)),
            dma((STEPS * 18 * (CHUNKS + 1),)),
            dma((8,)),
            dma((STEPS * 8,)),
            dma((9,)),
            dma((18,)),
            dma((14,)),
            dma((STEPS,)),
        ],
        compiler_params=pltpu.CompilerParams(
            collective_id=0, has_side_effects=True, vmem_limit_bytes=56 << 20
        ),
        cost_estimate=pl.CostEstimate(flops=10**10, bytes_accessed=7 << 20, transcendentals=0),
    )(matrix.reshape(4 * N, 128), pivots, lower_inv, upper_inv)
    return done.reshape(matrix.shape)


def solution(mesh):
    placed = (P(None, "prow", None, "pcol"), P(), P(), P())
    return jax.shard_map(
        body, mesh=mesh, in_specs=placed, out_specs=P(None, "prow", None, "pcol"), check_vma=False
    )
```
